32 devices in a mesh: fsdp: 8 (over z, core), ctx: 2 (over x), tp: 2 (over y).
Axes of the slice: x: 2, y: 2, z: 4, core: 2. Of those that a mesh axis runs over, the one named last changes fastest.
Arguments:
- tokens: bfloat16 [9216, 768], P(('fsdp', 'ctx')), may hold values from -6 to 6
- norm1_gain: bfloat16 [768], P('fsdp'), may hold values from 0.5 to 1.5
- w_qkv: bfloat16 [768, 3, 768], P('fsdp', None, 'tp'), may hold values from -0.21875 to 0.21875
- w_out: bfloat16 [768, 768], P('tp', 'fsdp'), may hold values from -0.875 to 0.875
- rel_bias: bfloat16 [32, 12], P('fsdp', 'tp'), may hold values from -3 to 3
- norm2_gain: bfloat16 [768], P('fsdp'), may hold values from 0.5 to 1.5
- w_up: bfloat16 [8, 768, 3072], P('fsdp', 'ctx', 'tp'), may hold values from -0.21875 to 0.21875
- w_down: bfloat16 [8, 3072, 768], P('fsdp', 'tp', 'ctx'), may hold values from -0.109375 to 0.109375
- gates: float32 [9216, 2], P(('fsdp', 'ctx')), may hold values from 0.2 to 0.8
- routes: int32 [9216, 2], P(('fsdp', 'ctx')), may hold values from 0 to 7, all different within a row; in each aligned block of 576 rows (0 to 575, 576 to 1151, ...) at most 288 rows name the same one
- lengths: int32 [8, 3], P('fsdp'), may hold values from 1 to 1024, 1152 in all within a row
- buckets: int32 [1152], replicated, may hold values from 0 to 31
- grad_out: float32 [9216, 768], P(('fsdp', 'ctx')), may hold values from -6 to 6
Outputs:
- output: float32 [9216, 768], P(('fsdp', 'ctx'))
- grad_tokens: float32 [9216, 768], P(('fsdp', 'ctx'))
- grad_norm1_gain: float32 [768], P('fsdp')
- grad_w_qkv: float32 [768, 3, 768], P('fsdp', None, 'tp')
- grad_w_out: float32 [768, 768], P('tp', 'fsdp')
- grad_rel_bias: float32 [32, 12], P('fsdp', 'tp')
- grad_norm2_gain: float32 [768], P('fsdp')
- grad_w_up: float32 [8, 768, 3072], P('fsdp', 'ctx', 'tp')
- grad_w_down: float32 [8, 3072, 768], P('fsdp', 'tp', 'ctx')
The draws below stay inside these ranges and needn't reach their ends.
Inputs may be any that keep to these rules, and one draw needn't show every extreme that they name: `routes`: each row names 2 different experts; in the rows of one device (aligned blocks of 576 rows) no expert is named more than 288 times. `lengths`: each row sums to 1152; its largest entry is 1024.
All inputs are finite; a program needn't handle non-finite values.
Results may differ from the reference program's by a relative error of at most 0.02.
Values may be sent and summed in bfloat16 or wider, within the bound.
A program may use at most 192 MiB of HBM per device.

```python
import math
import jax
import jax.numpy as jnp
import numpy as np
from jax import lax

D = 768
HEADS = 12
HEAD_DIM = 64
FF = 3072
BUCKETS = 32
TOP = 2
MAXLEN = 1024
EXPERTS = 8
GROUP = 1152
TOK_DEV = 576
TOKENS = 9216
CAP = 288
N_FSDP = 8
N_CTX = 2


def place_ends(entries, stream_key, least, largest):
    place = [jax.random.randint(jax.random.fold_in(stream_key, axis), (), 0, length) for axis, length in enumerate(entries.shape)]
    widest = entries.shape.index(max(entries.shape))
    next_to = place[:widest] + [(place[widest] + 1) % entries.shape[widest]] + place[widest + 1:]
    return entries.at[tuple(place)].set(least).at[tuple(next_to)].set(largest)


def shard_levels(stream_key, shape, shards, smallest, high):
    gain = 1.0
    for position, shards_of in shards:
        steps = jax.random.uniform(jax.random.fold_in(jax.random.fold_in(stream_key, 6), position), (shards_of,), jnp.float32, smallest / len(shards), high / len(shards))
        gain = gain * jnp.repeat(jnp.exp(steps), shape[position] // shards_of).reshape((-1,) + (1,) * (len(shape) - 1 - position))
    return gain


def length_profile(count, total, most, slope):
    portions = [(1 << 20) // math.isqrt(rank ** slope) + 1 for rank in range(2, count + 1)]
    rest, counts = total - most - (count - 1), [1] * (count - 1)
    while rest > 0:
        candidates = [i for i in range(count - 1) if counts[i] < most]
        whole, budget = sum([portions[i] for i in candidates]), rest
        for i in candidates:
            addition = min(most - counts[i], max(1, budget * portions[i] // whole), rest)
            counts[i] = counts[i] + addition
            rest = rest - addition
    return np.array([most] + counts)


def ragged_sizes(own_key, amount, total, reach, skew):
    if amount == 2:
        one = jax.random.randint(own_key, (), max(1, total - reach), min(reach, total - 1) + 1)
        return jnp.stack([one, total - one])
    tallies = jnp.asarray(length_profile(amount, total, reach, skew), jnp.int32)
    twos = (amount - 1) // 2
    giver, sink = tallies[1:1 + 2 * twos:2], tallies[2:2 + 2 * twos:2]
    room = jnp.minimum(giver - 1, reach - sink)
    shifted = jax.random.randint(jax.random.fold_in(own_key, 1), (twos,), 0, 1 << 20) % (room + 1)
    tallies = tallies.at[1:1 + 2 * twos:2].set(giver - shifted).at[2:2 + 2 * twos:2].set(sink + shifted)
    return tallies[jax.random.permutation(jax.random.fold_in(own_key, 2), amount)]


def assign_block(key, own, number, rows, number_of, top, bound, skew):
    sequence = jax.random.permutation(key, number_of)
    packed, ordinary = load_shares(number_of, rows * top, bound, skew, True), load_shares(number_of, rows * top, bound, skew, False)
    places = jnp.arange(number_of)

    def named(sizes, turn):
        used = int((sizes > 0).sum())
        fixed = max(1, used // 4)
        passed = fixed + (places - fixed + turn * (used - fixed)) % max(1, number_of - fixed)
        return jnp.zeros((number_of,), jnp.int32).at[sequence[jnp.where(places < fixed, places, passed)]].set(jnp.asarray(sizes, jnp.int32))

    sizes = jnp.where(number % 4 == 0, named(packed, number // 4), named(ordinary, number - number // 4 - 1))
    mixed = jax.random.permutation(jax.random.fold_in(own, 3), number_of)
    donor, receiver = mixed[0:number_of // 2 * 2:2], mixed[1:number_of // 2 * 2:2]
    slack = jnp.minimum(sizes[donor] - 1, bound - sizes[receiver]) // 2
    slack = jnp.where((donor == sequence[0]) | (receiver == sequence[0]) | (sizes[receiver] == 0), 0, jnp.maximum(slack, 0))
    passed = jax.random.randint(jax.random.fold_in(own, 4), (number_of // 2,), 0, 1 << 20) % (slack + 1)
    sizes = sizes.at[donor].add(-passed).at[receiver].add(passed)
    items = jnp.searchsorted(jnp.cumsum(sizes), jnp.arange(rows * top), side="right").astype(jnp.int32)
    grid = items.reshape(top, rows).T
    grid = grid[jax.random.permutation(jax.random.fold_in(own, 1), rows)]
    turn = jax.random.randint(jax.random.fold_in(own, 2), (rows, 1), 0, top)
    return jnp.take_along_axis(grid, (jnp.arange(top)[None, :] + turn) % top, axis=1)


def load_shares(amount, total, reach, lean, full):
    loads = [(1 << 20) // math.isqrt(rank ** lean) + 1 for rank in range(1, amount + 1)]
    largest = reach if full else min(reach, max(-(-total // amount), total * loads[0] // sum(loads)))
    least = 1 if total - largest >= amount - 1 else 0
    holding, surplus = [largest] + [least] * (amount - 1), total - largest - least * (amount - 1)
    while surplus > 0:
        candidates = [i for i in range(1, amount) if holding[i] < largest] or [i for i in range(1, amount) if holding[i] < reach]
        mass, remaining = sum([loads[i] for i in candidates]), surplus
        for i in candidates:
            extra = min(reach - holding[i], max(1, remaining * loads[i] // mass), surplus)
            holding[i] = holding[i] + extra
            surplus = surplus - extra
    return np.array(holding)


def scatter_about(stream_key, shape, width, bound, pieces=(), held_as=jnp.bfloat16):
    result = jax.random.normal(stream_key, shape, jnp.float32) * width
    if len(pieces) > 0:
        result = shard_levels(stream_key, shape, pieces, -0.22, 0.18) * result
    return jnp.clip(result, min=-bound, max=bound).astype(held_as)


def setup_inputs(seed: int = 0) -> dict:
    streams_of = jax.random.split(jax.random.key(seed), 14)
    tokens = scatter_about(streams_of[0], (TOKENS, D), 1.0, 6.0, ((0, 16),))
    norm1_gain = jnp.clip(1.0 + 0.1 * jax.random.normal(streams_of[1], (D,), jnp.float32), 0.5, 1.5).astype(jnp.bfloat16)
    w_qkv = scatter_about(streams_of[2], (D, 3, D), D ** -0.5, 0.21875, ((0, 8), (2, 2)))
    w_out = scatter_about(streams_of[3], (D, D), (D // 16) ** -0.5, 0.875, ((0, 2), (1, 8)))
    rel_bias = scatter_about(streams_of[4], (BUCKETS, HEADS), 0.5, 3.0, ((0, 8), (1, 2)))
    norm2_gain = jnp.clip(1.0 + 0.1 * jax.random.normal(streams_of[5], (D,), jnp.float32), 0.5, 1.5).astype(jnp.bfloat16)
    w_up = scatter_about(streams_of[6], (EXPERTS, D, FF), D ** -0.5, 0.21875, ((0, 8), (1, 2), (2, 2)))
    w_down = scatter_about(streams_of[7], (EXPERTS, FF, D), FF ** -0.5, 0.109375, ((0, 8), (1, 2), (2, 2)))
    gates = jnp.clip(0.2 + 0.6 * jax.random.uniform(streams_of[8], (TOKENS, TOP), jnp.float32) ** shard_levels(streams_of[8], (TOKENS, TOP), ((0, 16),), -0.2, 0.2), 0.2, 0.8)
    routes_keys = jax.random.split(jax.random.fold_in(streams_of[9], 1), TOKENS // TOK_DEV)
    routes_turns = jax.random.permutation(jax.random.fold_in(streams_of[9], 3), TOKENS // TOK_DEV)
    routes = jax.vmap(lambda own, number: assign_block(jax.random.fold_in(streams_of[9], 2), own, number, TOK_DEV, EXPERTS, TOP, CAP, 2))(routes_keys, routes_turns).reshape((TOKENS, TOP))
    lengths = jax.vmap(lambda own: ragged_sizes(own, 3, GROUP, MAXLEN, 2))(jax.random.split(streams_of[10], N_FSDP)).reshape((N_FSDP, 3)).astype(jnp.int32)
    buckets = place_ends(jax.random.randint(streams_of[11], (GROUP,), 0, BUCKETS), jax.random.fold_in(streams_of[11], 1), 0, BUCKETS - 1).astype(jnp.int32)
    grad_out = scatter_about(streams_of[12], (TOKENS, D), 1.0, 6.0, ((0, 16),), jnp.float32)
    return dict(tokens=tokens, norm1_gain=norm1_gain, w_qkv=w_qkv, w_out=w_out, rel_bias=rel_bias, norm2_gain=norm2_gain, w_up=w_up, w_down=w_down, gates=gates, routes=routes, lengths=lengths, buckets=buckets, grad_out=grad_out)


eps = 1e-06

@jax.custom_vjp
def low(v):
    return lax.optimization_barrier(v.astype(jnp.bfloat16)).astype(jnp.float32)

@jax.custom_vjp
def low_back(v):
    return v

def low_keep(v):
    return (low(v), None)

def low_pass(kept, grad):
    return (grad,)

def back_keep(v):
    return (v, None)

def back_low(kept, grad):
    return (low(grad),)
low.defvjp(low_keep, low_pass)
low_back.defvjp(back_keep, back_low)

def norm_rows(values, gain_vec):
    factor = lax.rsqrt(lax.optimization_barrier(jnp.mean(values * values, axis=-1, keepdims=True)) + eps)
    return values * factor * gain_vec

def attend_group(bias_dist, queries, keys_in, values_in, seq_lengths):
    positions = jnp.arange(GROUP, dtype=jnp.int32)
    seq_ends = jnp.cumsum(seq_lengths).astype(jnp.int32)
    seq_ident = lax.optimization_barrier(jnp.sum((positions[:, None] >= seq_ends[None, :]).astype(jnp.int32), axis=1)).astype(jnp.int32)
    allowed = (seq_ident[:, None] == seq_ident[None, :]) & (positions[None, :] <= positions[:, None])
    distance = jnp.maximum(positions[:, None] - positions[None, :], 0).astype(jnp.int32)
    bias_full = jnp.transpose(bias_dist[distance], (2, 0, 1))
    scores = jnp.einsum('qhd,khd->hqk', queries, keys_in, precision=lax.Precision.HIGHEST) * HEAD_DIM ** (-0.5) + bias_full
    scores = low_back(scores)
    scores = jnp.where(allowed[None], scores, -1e+30)
    highest = lax.optimization_barrier(jnp.max(scores, axis=-1, keepdims=True))
    weights = jnp.exp(scores - highest)
    attn_probs = weights / lax.optimization_barrier(jnp.sum(weights, axis=-1, keepdims=True))
    return jnp.einsum('hqk,khd->qhd', low(attn_probs), values_in, precision=lax.Precision.HIGHEST)

def route_slots(routes):
    block_count = N_FSDP * N_CTX
    blocks = routes.reshape(block_count, TOK_DEV * TOP)
    onehot = (blocks[:, :, None] == jnp.arange(EXPERTS, dtype=jnp.int32)[None, None, :]).astype(jnp.int32)
    slot_place = lax.optimization_barrier(jnp.sum((jnp.cumsum(onehot, axis=1).astype(jnp.int32) - 1) * onehot, axis=2)).astype(jnp.int32)
    source = jnp.arange(block_count, dtype=jnp.int32)[:, None]
    slot_index = blocks * (block_count * CAP) + source * CAP + slot_place
    token_index = source * TOK_DEV + jnp.arange(TOK_DEV * TOP, dtype=jnp.int32)[None, :] // TOP
    return (slot_index.reshape(-1).astype(jnp.int32), token_index.reshape(-1).astype(jnp.int32))

def expert_block(expert_item):
    rows_in, up_one, down_one = expert_item
    inner_act = low_back(jnp.dot(rows_in, up_one, precision=lax.Precision.HIGHEST))
    hidden = low(jax.nn.gelu(inner_act))
    return low(low_back(jnp.dot(hidden, down_one, precision=lax.Precision.HIGHEST)))

def reference(tokens, norm1_gain, w_qkv, w_out, rel_bias, norm2_gain, w_up, w_down, gates, routes, lengths, buckets, grad_out):
    slot_index, token_index = route_slots(routes)
    slot_total = EXPERTS * N_FSDP * N_CTX * CAP
    owner = jnp.zeros((slot_total,), jnp.int32).at[slot_index].set(token_index)
    filled = jnp.zeros((slot_total,), jnp.float32).at[slot_index].set(1.0)
    gate_flat = gates.reshape(-1)

    def forward(inputs, gain_one, qkv_weight, out_weight, bias_table, gain_two, up_weight, down_weight):
        normed = low(norm_rows(inputs, gain_one))
        project = jnp.dot(normed, qkv_weight.reshape(D, 3 * D), precision=lax.Precision.HIGHEST)
        project = low(low_back(project)).reshape(N_FSDP, GROUP, 3, HEADS, HEAD_DIM)
        bias_dist = bias_table[buckets]

        def attend_one(group_item):
            return attend_group(bias_dist, group_item[0], group_item[1], group_item[2], group_item[3])
        attended = lax.map(jax.checkpoint(attend_one), (project[:, :, 0], project[:, :, 1], project[:, :, 2], lengths))
        attended = low(low_back(attended.reshape(TOKENS, D)))
        attn_branch = low_back(jnp.dot(attended, out_weight, precision=lax.Precision.HIGHEST))
        middle = inputs + attn_branch
        normed_two = low(norm_rows(middle, gain_two))
        rows_all = low_back(normed_two[owner] * filled[:, None]).reshape(EXPERTS, N_FSDP * N_CTX * CAP, D)
        expert_out = lax.map(jax.checkpoint(expert_block), (rows_all, up_weight, down_weight)).reshape(slot_total, D)
        mixture = jnp.zeros_like(middle).at[token_index].add(gate_flat[:, None] * expert_out[slot_index])
        return middle + mixture
    params = tuple((item.astype(jnp.float32) for item in (tokens, norm1_gain, w_qkv, w_out, rel_bias, norm2_gain, w_up, w_down)))
    output, pull = jax.vjp(forward, *params)
    grads = pull(grad_out)
    return (output, grads[0], grads[1], grads[2], grads[3], grads[4], grads[5], grads[6], grads[7])
```

```python
import functools

import jax
import jax.numpy as jnp
from jax import lax
from jax.experimental import pallas as pl
from jax.experimental.pallas import tpu as pltpu
from jax.sharding import PartitionSpec as P

HEAD_DIM = 64
TOP = 2
LANES = 128
eps = 1e-06
F32 = jnp.float32
BF16 = jnp.bfloat16
SCALE = HEAD_DIM ** (-0.5)
VMEM = 48 * 1024 * 1024


def dot(a, b, dims=((1,), (0,))):
    return lax.dot_general(a, b, (dims, ((), ())), preferred_element_type=F32)


NT = ((1,), (1,))
TN = ((0,), (0,))


def norm_forward(values, gain_vec):
    inverse = lax.rsqrt(jnp.mean(values * values, axis=-1, keepdims=True) + eps)
    normal = values * inverse
    return (normal * gain_vec, normal, inverse)


def norm_backward(upstream, gain_vec, normal, inverse):
    gain_grad = jnp.sum(upstream * normal, axis=0)
    scaled = upstream * gain_vec
    input_grad = inverse * (scaled - normal * jnp.mean(scaled * normal, axis=-1, keepdims=True))
    return (input_grad, gain_grad)


def round_low(x):
    return lax.reduce_precision(x.astype(F32), 8, 7).astype(BF16)


def swap(x, axis):
    return lax.ppermute(x, axis, [(0, 1), (1, 0)])


def in_order(mine, other, index, axis):
    return jnp.where(
        index == 0,
        jnp.concatenate((mine, other), axis=axis),
        jnp.concatenate((other, mine), axis=axis),
    )


def gather_axis(x, name, axis):
    if lax.axis_size(name) == 2:
        return in_order(x, swap(x, name), lax.axis_index(name), axis)
    return lax.all_gather(x, name, axis=axis, tiled=True)


def scatter_axis(x, name, axis):
    if lax.axis_size(name) == 2:
        size = x.shape[axis] // 2
        index = lax.axis_index(name)
        away = lax.dynamic_slice_in_dim(x, (1 - index) * size, size, axis)
        kept = lax.dynamic_slice_in_dim(x, index * size, size, axis)
        return kept.astype(F32) + swap(away.astype(BF16), name).astype(F32)
    return lax.psum_scatter(x.astype(BF16), name, scatter_dimension=axis, tiled=True).astype(F32)


def sum_axis(x, name):
    if lax.axis_size(name) == 2:
        return x.astype(F32) + swap(x, name).astype(F32)
    return lax.psum(x, name).astype(F32)


def sibling(x):
    size = lax.axis_size("fsdp")
    return lax.ppermute(x, "fsdp", [(i, i ^ 1) for i in range(size)])


def line(x, chips, step):
    perm = [(2 * c + k, 2 * (c + step) + k) for c in chips for k in range(2)]
    return lax.ppermute(x, "fsdp", perm)


def line_gather(x):
    chips = lax.axis_size("fsdp") // 2
    chip = lax.axis_index("fsdp") // 2
    below, above = [], []
    up, down = x, x
    for s in range(1, chips):
        up = line(up, range(s - 1, chips - 1), 1)
        down = line(down, range(1, chips - s + 1), -1)
        below.append(up)
        above.append(down)
    every = jnp.stack(below[::-1] + [x] + above)
    mine = lax.dynamic_slice_in_dim(every, chips - 1 - chip, chips, 0)
    return mine, sibling(mine)


def line_scatter(mine, other):
    chips = lax.axis_size("fsdp") // 2
    chip = lax.axis_index("fsdp") // 2
    part = (mine.astype(F32) + sibling(other).astype(F32)).astype(BF16)
    up = down = None
    for t in range(1, chips):
        high = lax.dynamic_index_in_dim(part, jnp.minimum(chip + chips - t, chips - 1), 0, False)
        low = lax.dynamic_index_in_dim(part, jnp.maximum(chip - chips + t, 0), 0, False)
        if up is not None:
            high = (high.astype(F32) + up.astype(F32)).astype(BF16)
            low = (low.astype(F32) + down.astype(F32)).astype(BF16)
        up = line(high, range(0, t), 1)
        down = line(low, range(chips - t, chips), -1)
    own = lax.dynamic_index_in_dim(part, chip, 0, False)
    return own.astype(F32) + (up.astype(F32) + down.astype(F32))


def by_index(mine, other):
    core = lax.axis_index("fsdp") % 2
    return jnp.where(
        core == 0, jnp.stack((mine, other), axis=1), jnp.stack((other, mine), axis=1)
    )


def by_core(blocks):
    core = lax.axis_index("fsdp") % 2
    pairs = blocks.reshape((blocks.shape[0] // 2, 2) + blocks.shape[1:])
    return (
        jnp.where(core == 0, pairs[:, 0], pairs[:, 1]),
        jnp.where(core == 0, pairs[:, 1], pairs[:, 0]),
    )


def half_lanes(x, h):
    lane = lax.broadcasted_iota(jnp.int32, x.shape, 1)
    return jnp.where((lane >= HEAD_DIM) == (h == 1), x, jnp.zeros_like(x))


def join_lanes(a, b):
    lane = lax.broadcasted_iota(jnp.int32, a.shape, 1)
    return jnp.where(lane < HEAD_DIM, a, b)


def attend_kernel(tile, q_ref, k_ref, v_ref, vec_ref, lo_ref, hi_ref, o_ref, p_ref):
    rows, keys = q_ref.shape[0], k_ref.shape[0]
    k, v = k_ref[...], v_ref[...]
    place = lax.broadcasted_iota(jnp.int32, (tile, keys), 1)
    for start in range(0, rows, tile):
        at = pl.ds(start, tile)
        q = q_ref[at, :]
        allowed = (place >= lo_ref[at, :]) & (place <= hi_ref[at, :])
        outs = []
        for h in range(2):
            bias = pltpu.roll(
                jnp.broadcast_to(vec_ref[0, h : h + 1, :], (tile, keys)),
                start,
                1,
                stride=1,
                stride_axis=0,
            )
            s = dot(half_lanes(q, h), k, NT) * SCALE + bias
            s = jnp.where(allowed, s, -1e30)
            e = jnp.exp(s - jnp.max(s, axis=1, keepdims=True))
            p = (e * (1.0 / jnp.sum(e, axis=1, keepdims=True))).astype(BF16)
            p_ref[h, at, :] = p
            outs.append(dot(p, v))
        o_ref[at, :] = join_lanes(*outs).astype(BF16)


def attend_back_kernel(tile, q_ref, k_ref, v_ref, p_ref, go_ref, dq_ref, dk_ref, dv_ref, diag_ref):
    rows, keys = q_ref.shape[0], k_ref.shape[0]
    k, v = k_ref[...], v_ref[...]
    dk = [jnp.zeros((keys, LANES), F32) for _ in range(2)]
    dv = [jnp.zeros((keys, LANES), F32) for _ in range(2)]
    diag = [jnp.zeros((8, keys), F32) for _ in range(2)]
    for start in range(0, rows, tile):
        at = pl.ds(start, tile)
        q, go = q_ref[at, :], go_ref[at, :]
        dq = []
        for h in range(2):
            p_low = p_ref[h, at, :]
            p = p_low.astype(F32)
            dp = dot(half_lanes(go, h), v, NT)
            ds = p * (dp - jnp.sum(p * dp, axis=1, keepdims=True))
            low = ds.astype(BF16)
            dq.append(dot(low, k))
            dk[h] = dk[h] + dot(low, q, TN)
            dv[h] = dv[h] + dot(p_low, go, TN)
            while ds.shape[0] % 16 == 0:
                n = ds.shape[0] // 2
                ds = ds[:n] + pltpu.roll(ds[n:], keys - n, 1)
            total = ds[:8]
            for g in range(8, ds.shape[0], 8):
                total = total + pltpu.roll(ds[g : g + 8], keys - g, 1)
            if start:
                total = pltpu.roll(total, keys - start, 1)
            diag[h] = diag[h] + total
        dq_ref[at, :] = (join_lanes(*dq) * SCALE).astype(BF16)
    dk_ref[...] = (join_lanes(*dk) * SCALE).astype(BF16)
    dv_ref[...] = join_lanes(*dv).astype(BF16)
    for h in range(2):
        diag_ref[0, h] = diag[h]


def row_tile(rows):
    return 192 if rows % 192 == 0 else rows


def attend(project, kv, vec, lo, hi):
    rows, keys = project.shape[0], kv.shape[0]
    pairs = kv.shape[1] // 2 // LANES
    column = lambda shift: lambda g: (0, g + shift)
    return pl.pallas_call(
        functools.partial(attend_kernel, row_tile(rows)),
        grid=(pairs,),
        in_specs=[
            pl.BlockSpec((rows, LANES), column(0)),
            pl.BlockSpec((keys, LANES), column(0)),
            pl.BlockSpec((keys, LANES), column(pairs)),
            pl.BlockSpec((1, 2, keys), lambda g: (g, 0, 0)),
            pl.BlockSpec((rows, 1), lambda g: (0, 0)),
            pl.BlockSpec((rows, 1), lambda g: (0, 0)),
        ],
        out_specs=[
            pl.BlockSpec((rows, LANES), column(0)),
            pl.BlockSpec((2, rows, keys), lambda g: (g, 0, 0)),
        ],
        out_shape=[
            jax.ShapeDtypeStruct((rows, pairs * LANES), BF16),
            jax.ShapeDtypeStruct((2 * pairs, rows, keys), BF16),
        ],
        compiler_params=pltpu.CompilerParams(vmem_limit_bytes=VMEM),
        cost_estimate=pl.CostEstimate(
            flops=8 * pairs * rows * keys * LANES,
            bytes_accessed=4 * pairs * rows * keys,
            transcendentals=2 * pairs * rows * keys,
        ),
        name="attend",
    )(project, kv, kv, vec.reshape(pairs, 2, keys), lo, hi)


def attend_back(project, kv, probs, go):
    rows, keys = project.shape[0], kv.shape[0]
    pairs = kv.shape[1] // 2 // LANES
    column = lambda shift: lambda g: (0, g + shift)
    return pl.pallas_call(
        functools.partial(attend_back_kernel, row_tile(rows)),
        grid=(pairs,),
        in_specs=[
            pl.BlockSpec((rows, LANES), column(0)),
            pl.BlockSpec((keys, LANES), column(0)),
            pl.BlockSpec((keys, LANES), column(pairs)),
            pl.BlockSpec((2, rows, keys), lambda g: (g, 0, 0)),
            pl.BlockSpec((rows, LANES), column(0)),
        ],
        out_specs=[
            pl.BlockSpec((rows, LANES), column(0)),
            pl.BlockSpec((keys, LANES), column(0)),
            pl.BlockSpec((keys, LANES), column(0)),
            pl.BlockSpec((1, 2, 8, keys), lambda g: (g, 0, 0, 0)),
        ],
        out_shape=[
            jax.ShapeDtypeStruct((rows, pairs * LANES), BF16),
            jax.ShapeDtypeStruct((keys, pairs * LANES), BF16),
            jax.ShapeDtypeStruct((keys, pairs * LANES), BF16),
            jax.ShapeDtypeStruct((pairs, 2, 8, keys), F32),
        ],
        compiler_params=pltpu.CompilerParams(vmem_limit_bytes=VMEM),
        cost_estimate=pl.CostEstimate(
            flops=16 * pairs * rows * keys * LANES,
            bytes_accessed=4 * pairs * rows * keys,
            transcendentals=0,
        ),
        name="attend_back",
    )(project, kv, kv, probs, go)


def expert(rows, grads, up, down):
    out = back = 0.0
    up_grad, down_grad = [], []
    for f in range(2):
        inner, pull = jax.vjp(jax.nn.gelu, dot(rows, up[f]))
        hidden = inner.astype(BF16)
        inner_grad = pull(dot(grads, down[f], NT))[0].astype(BF16)
        out = out + dot(hidden, down[f])
        back = back + dot(inner_grad, up[f], NT)
        up_grad.append(dot(rows, inner_grad, TN).astype(BF16))
        down_grad.append(dot(hidden, grads, TN).astype(BF16))
    return out.astype(BF16), back.astype(BF16), up_grad, down_grad


def body(
    tokens,
    norm1_gain,
    w_qkv,
    w_out,
    rel_bias,
    norm2_gain,
    w_up,
    w_down,
    gates,
    routes,
    lengths,
    buckets,
    grad_out,
):
    count, width = tokens.shape
    ctx_index, tp_index = lax.axis_index("ctx"), lax.axis_index("tp")
    ctx_size, fsdp_size = lax.axis_size("ctx"), lax.axis_size("fsdp")
    group_len = count * ctx_size
    half = count // 2
    feat = w_qkv.shape[2]
    heads = feat // HEAD_DIM
    share = w_qkv.shape[0]
    bias_rows = rel_bias.shape[0]
    buckets_all = bias_rows * fsdp_size
    mine = lambda x: lax.dynamic_slice_in_dim(x, tp_index * half, half, 0)

    small = jnp.zeros((share, LANES), BF16)
    small = small.at[:, 0].set(norm1_gain).at[:, 1].set(norm2_gain)
    small = small.at[:bias_rows, 2 : 2 + heads].set(rel_bias)
    packed = jnp.concatenate((w_qkv.reshape(share, 3 * feat), w_out.T, small), axis=1)
    packed = by_index(*line_gather(packed)).reshape(fsdp_size * share, packed.shape[1])
    qkv_weight = packed[:, : 3 * feat]
    out_weight = packed[:, 3 * feat : 4 * feat]
    small = packed[:, 4 * feat :]
    gain_one, gain_two = small[:, 0].astype(F32), small[:, 1].astype(F32)
    table = small[:, 2 : 2 + heads].reshape(fsdp_size, share, heads)[:, :bias_rows]
    table = table.reshape(buckets_all, heads)

    up_mine = gather_axis(w_up[0], "ctx", 0)
    up = (up_mine, swap(up_mine, "tp"))
    down = jnp.concatenate((w_down[0], swap(w_down[0], "tp")), axis=0)
    down = gather_axis(down, "ctx", 1)
    hidden = w_down.shape[1]
    down = (down[:hidden], down[hidden:])

    extra = jnp.concatenate((routes.astype(BF16), gates.astype(BF16)), axis=1)
    extra = jnp.pad(extra, ((0, 0), (0, LANES - 2 * TOP)))
    told = mine(jnp.concatenate((grad_out.astype(BF16), extra), axis=1))

    inputs = tokens.astype(F32)
    normed_low = norm_forward(inputs, gain_one)[0].astype(BF16)
    project = dot(normed_low, qkv_weight).astype(BF16)
    kv = gather_axis(project[:, feat:], "ctx", 0)
    start = ctx_index * count
    hi = start + jnp.arange(count, dtype=jnp.int32)
    ends = jnp.cumsum(lengths[0])
    lo = jnp.max(jnp.where(hi[:, None] >= ends[None, :], ends[None, :], 0), axis=1)
    flipped = buckets[::-1]
    turned = lax.dynamic_slice_in_dim(
        jnp.concatenate((flipped, flipped)), group_len - 1 - start, group_len
    )
    hot = (turned[None, :] == jnp.arange(buckets_all, dtype=jnp.int32)[:, None]).astype(BF16)
    vec = dot(table, hot, TN)
    attended, probs = attend(project, kv, vec, lo[:, None], hi[:, None])
    branch = dot(attended, out_weight, NT).astype(BF16)
    middle = mine(inputs) + scatter_axis(branch, "tp", 0)
    normed_two, normal_two, inverse_two = norm_forward(middle, gain_two)

    told = jnp.concatenate(line_gather(told), axis=0).reshape(fsdp_size * half, -1)
    rows = jnp.concatenate(line_gather(normed_two.astype(BF16)), axis=0)
    rows = rows.reshape(fsdp_size * half, width)
    expert_index = lax.axis_index("fsdp").astype(F32)
    named = told[:, width : width + TOP].astype(F32) == expert_index
    gate = jnp.where(named, told[:, width + TOP : width + 2 * TOP].astype(F32), 0.0)
    gate = jnp.sum(gate, axis=1, keepdims=True)
    grads = (gate * told[:, :width].astype(F32)).astype(BF16)
    chosen = jnp.any(named, axis=1)
    order = jnp.cumsum(chosen.astype(jnp.int32)) - 1
    total = rows.shape[0]
    room = -(-(4 * TOP * total) // (3 * fsdp_size * LANES)) * LANES
    room = min(room, total)

    def few(rows, grads, order, chosen):
        pick = (
            (order[None, :] == jnp.arange(room, dtype=jnp.int32)[:, None]) & chosen[None, :]
        ).astype(BF16)
        out, back, up_grad, down_grad = expert(
            dot(pick, rows).astype(BF16), dot(pick, grads).astype(BF16), up, down
        )
        spread = lambda x: dot(pick, x, TN).astype(BF16)
        return spread(out), spread(back), up_grad, down_grad

    def many(rows, grads, order, chosen):
        return expert(rows, grads, up, down)

    expert_out, row_grad, up_grad, down_grad = lax.cond(
        jnp.sum(chosen.astype(jnp.int32)) <= room, few, many, rows, grads, order, chosen
    )
    row_grad = jnp.where(chosen[:, None], row_grad, jnp.zeros_like(row_grad))
    expert_out = (gate * expert_out.astype(F32)).astype(BF16)
    lines = lambda x: x.reshape(2, fsdp_size // 2, half, width)
    row_grad, expert_out = lines(row_grad), lines(expert_out)
    grad_normed_two = line_scatter(row_grad[0], row_grad[1])
    mixture = line_scatter(expert_out[0], expert_out[1])
    output = gather_axis(round_low(middle + mixture), "tp", 0).astype(F32)

    up_sum = up_grad[0].astype(F32) + swap(up_grad[1], "tp").astype(F32)
    grad_up = scatter_axis(up_sum, "ctx", 0)[None]
    down_sum = scatter_axis(jnp.stack(down_grad), "ctx", 2)
    grad_down = (down_sum[0] + swap(down_sum[1].astype(BF16), "tp").astype(F32))[None]

    grad_from_two, gain_two_grad = norm_backward(grad_normed_two, gain_two, normal_two, inverse_two)
    grad_middle = mine(grad_out) + grad_from_two
    grad_branch = gather_axis(grad_middle.astype(BF16), "tp", 0)
    grad_attended = dot(grad_branch, out_weight).astype(BF16)
    grad_q, grad_k, grad_v, diag = attend_back(project, kv, probs, grad_attended)
    grad_out_weight = dot(grad_branch, attended, TN)
    kv_mine = scatter_axis(jnp.concatenate((grad_k, grad_v), axis=1), "ctx", 0)
    project_grad = jnp.concatenate((grad_q, kv_mine.astype(BF16)), axis=1)
    grad_normed_one = scatter_axis(dot(project_grad, qkv_weight, NT).astype(BF16), "tp", 0)
    grad_qkv = dot(normed_low, project_grad, TN)
    _, normal_one, inverse_one = norm_forward(mine(inputs), gain_one)
    grad_from_one, gain_one_grad = norm_backward(grad_normed_one, gain_one, normal_one, inverse_one)
    grad_input = gather_axis(round_low(grad_middle + grad_from_one), "tp", 0).astype(F32)

    diag = diag.reshape(heads, 8, group_len)
    diag = sum(jnp.roll(diag[:, r], -r, axis=1) for r in range(8))
    bias_grad = lax.dot_general(
        hot.astype(F32), diag, (NT, ((), ())), precision=lax.Precision.HIGHEST
    )
    gain_grads = jnp.stack((gain_one_grad, gain_two_grad), axis=1)
    gain_grads = gain_grads + swap(gain_grads, "tp")
    bias_grad = bias_grad.reshape(fsdp_size, bias_rows, heads)
    bias_grad = jnp.pad(bias_grad, ((0, 0), (0, share - bias_rows), (0, 0)))
    small = jnp.concatenate((gain_grads, bias_grad.reshape(-1, heads)), axis=1)
    small = jnp.pad(small, ((0, 0), (0, LANES - 2 - heads)))
    packed = jnp.concatenate(
        (grad_qkv.astype(BF16), grad_out_weight.astype(BF16), small.astype(BF16)), axis=1
    ).reshape(fsdp_size, share, -1)
    packed = sum_axis(round_low(line_scatter(*by_core(packed))), "ctx")
    return (
        output,
        grad_input,
        packed[:, 4 * feat],
        packed[:, : 3 * feat].reshape(share, 3, feat),
        packed[:, 3 * feat : 4 * feat].T,
        packed[:bias_rows, 4 * feat + 2 : 4 * feat + 2 + heads],
        packed[:, 4 * feat + 1],
        grad_up,
        grad_down,
    )


def solution(mesh):
    in_specs = (
        P(("fsdp", "ctx"), None),
        P("fsdp"),
        P("fsdp", None, "tp"),
        P("tp", "fsdp"),
        P("fsdp", "tp"),
        P("fsdp"),
        P("fsdp", "ctx", "tp"),
        P("fsdp", "tp", "ctx"),
        P(("fsdp", "ctx"), None),
        P(("fsdp", "ctx"), None),
        P("fsdp", None),
        P(),
        P(("fsdp", "ctx"), None),
    )
    out_specs = (
        P(("fsdp", "ctx"), None),
        P(("fsdp", "ctx"), None),
        P("fsdp"),
        P("fsdp", None, "tp"),
        P("tp", "fsdp"),
        P("fsdp", "tp"),
        P("fsdp"),
        P("fsdp", "ctx", "tp"),
        P("fsdp", "tp", "ctx"),
    )
    return jax.shard_map(body, mesh=mesh, in_specs=in_specs, out_specs=out_specs, check_vma=False)
```
